256 devices in a mesh: dp: 4 (over z_lo), fsdp: 64 (over y, x, z_hi, core).
Axes of the slice: x: 4, y: 4, z: 8 (z_hi: 2, z_lo: 4; z = z_hi * 4 + z_lo), core: 2. Of those that a mesh axis runs over, the one named last changes fastest.
Arguments:
- normed: bfloat16 [65536, 4608], P(('dp', 'fsdp')), may hold values from -6 to 6
- key_weight: bfloat16 [4608, 1024], P('fsdp'), may hold values from -0.09375 to 0.09375
- key_grad: bfloat16 [65536, 1024], P(('dp', 'fsdp')), may hold values from -6 to 6
Outputs:
- keys: bfloat16 [65536, 1024], P(('dp', 'fsdp'))
- input_grad: bfloat16 [65536, 4608], P(('dp', 'fsdp'))
- weight_grad: float32 [4608, 1024], P('fsdp')
The draws below stay inside these ranges and needn't reach their ends.
All inputs are finite; a program needn't handle non-finite values.
Results may differ from the reference program's by a relative error of at most 0.004.
Values may be sent and summed in bfloat16 or wider, within the bound.
No kernel may reach another device: no remote copies, remote signals or barrier semaphores. Data moves between devices by JAX's collectives and lax.ppermute only.
A program may use at most 128 MiB of HBM per device.

```python
import jax
import jax.numpy as jnp
from jax import lax

D = 4608
GROUP = 128
TAIL = 32
TOK_DEV = 256
KD = 1024
TOKENS = 65536


def levels(rng, extent, cuts, smallest, top_value):
    gain, own = 1.0, jax.random.fold_in(rng, 6)
    for axis_at, parts in cuts:
        heights = jnp.exp(jax.random.uniform(jax.random.fold_in(own, axis_at), (parts,), jnp.float32, smallest / len(cuts), top_value / len(cuts)))
        gain = gain * jnp.repeat(heights, extent[axis_at] // parts).reshape([-1 if axis == axis_at else 1 for axis in range(len(extent))])
    return gain


def normal_values(own_key, dims, deviation, bound, cuts=(), kind=jnp.bfloat16):
    values = deviation * jax.random.normal(own_key, dims, jnp.float32)
    if cuts:
        values = values * levels(own_key, dims, cuts, -0.22, 0.18)
    return jnp.clip(values, -bound, bound).astype(kind)


def setup_inputs(seed: int = 0) -> dict:
    splits = jax.random.split(jax.random.key(seed), 4)
    return {
        "normed": normal_values(splits[0], (TOKENS, D), 1.0, 6.0, ((0, 256),)),
        "key_weight": normal_values(splits[1], (D, KD), D ** -0.5, 0.09375, ((0, 64),)),
        "key_grad": normal_values(splits[2], (TOKENS, KD), 1.0, 6.0, ((0, 256),)),
    }


def restore(normed, block):
    rows, width = normed.shape
    values = normed.astype(jnp.float32).reshape(rows, width // GROUP, GROUP)
    scale = jnp.max(jnp.abs(values), axis=-1, keepdims=True)
    code = (2.0 * values >= -scale).astype(jnp.float32) + (values >= 0.0).astype(jnp.float32) + (2.0 * values >= scale).astype(jnp.float32)
    approx = ((code - 1.5) * 0.5 * scale).reshape(rows, width).astype(jnp.bfloat16)
    position = jnp.arange(rows, dtype=jnp.int32) % block
    exact = (position >= block - TAIL)[:, None]
    return jnp.where(exact, normed, approx)


def reference(normed, key_weight, key_grad):
    keys = jnp.dot(normed, key_weight, preferred_element_type=jnp.float32).astype(jnp.bfloat16)
    input_grad = lax.dot_general(key_grad, key_weight, (((1,), (1,)), ((), ())), preferred_element_type=jnp.float32).astype(jnp.bfloat16)
    restored = restore(normed, TOK_DEV)
    weight_grad = lax.dot_general(restored, key_grad, (((0,), (0,)), ((), ())), preferred_element_type=jnp.float32)
    return keys, input_grad, weight_grad
```

```python
import jax
import jax.numpy as jnp
from jax import lax
from jax.experimental import pallas as pl
from jax.experimental.pallas import tpu as pltpu
from jax.sharding import Mesh, PartitionSpec as P

GROUP = 128
TAIL = 32
AXES = ("zl", "y", "x", "zh", "c")
SIZES = (4, 4, 4, 2, 2)
TOK = 256
D = 4608
KD = 1024
HALF = KD // 2
BLK = D // 16
VMEM_LIMIT = 48 * 1024 * 1024


def pairs(move):
    out = []
    for i in range(256):
        rest, at = i, {}
        for name, size in zip(reversed(AXES), reversed(SIZES)):
            at[name] = rest % size
            rest //= size
        to = move(dict(at))
        j = 0
        for name, size in zip(AXES, SIZES):
            j = j * size + to[name] % size
        out.append((i, j))
    return out


def send(value, move):
    return lax.ppermute(value, AXES, pairs(move))


def other_core(at):
    at["c"] ^= 1
    return at


def mirror(at):
    at["zh"] ^= 1
    at["zl"] = 3 - at["zl"]
    return at


def first_by(step):
    def move(at):
        at["x" if at["c"] == 0 else "y"] += step
        return at

    return move


def second_by(step):
    def move(at):
        at["y" if at["c"] == 0 else "x"] += step
        return at

    return move


def zl_by(step):
    def move(at):
        at["zl"] += step
        return at

    return move


def quantize_kernel(x_ref, out_ref):
    for g in range(x_ref.shape[1] // GROUP):
        v = x_ref[:, g * GROUP : (g + 1) * GROUP].astype(jnp.float32).T
        scale = jnp.max(jnp.abs(v), axis=0, keepdims=True)
        low = (0.25 * scale).astype(jnp.bfloat16).astype(jnp.float32)
        high = (0.75 * scale).astype(jnp.bfloat16).astype(jnp.float32)
        twice = v + v
        mag = jnp.where((twice >= scale) | (twice < -scale), high, low)
        r = jnp.where(v >= 0.0, mag, -mag)
        token = lax.broadcasted_iota(jnp.int32, r.shape, 1)
        r = jnp.where(token >= TOK - TAIL, v, r)
        out_ref[g * GROUP : (g + 1) * GROUP, :] = r.astype(jnp.bfloat16)


def quantize(normed):
    width = 4 * GROUP
    return pl.pallas_call(
        quantize_kernel,
        grid=(D // width,),
        in_specs=[pl.BlockSpec((TOK, width), lambda i: (0, i))],
        out_specs=pl.BlockSpec((width, TOK), lambda i: (i, 0)),
        out_shape=jax.ShapeDtypeStruct((D, TOK), jnp.bfloat16),
        compiler_params=pltpu.CompilerParams(vmem_limit_bytes=VMEM_LIMIT),
        cost_estimate=pl.CostEstimate(flops=0, bytes_accessed=4 * D * TOK, transcendentals=0),
    )(normed)


def partial_kernel(at_ref, mine_ref, theirs_ref, gmine_ref, gtheirs_ref, o0, o1, o2, o3, acc, sem):
    step = pl.program_id(0)
    rows = mine_ref.shape[0]
    total = jnp.dot(mine_ref[...], gmine_ref[...], preferred_element_type=jnp.float32)
    total += jnp.dot(theirs_ref[...], gtheirs_ref[...], preferred_element_type=jnp.float32)
    acc[pl.ds(pl.multiple_of(step * rows, rows), rows), :] = total.astype(jnp.bfloat16)

    @pl.when(step == pl.num_programs(0) - 1)
    def _():
        first, core = at_ref[0], at_ref[2]
        copies = []
        for j, out in enumerate((o0, o1, o2, o3)):
            to = lax.rem(first + j, 4)
            for i in range(4):
                block = jnp.where(core == 0, 4 * i + to, 4 * to + i)
                copy = pltpu.make_async_copy(
                    acc.at[pl.ds(pl.multiple_of(block * BLK, BLK), BLK), :], out.at[i], sem.at[j, i]
                )
                copy.start()
                copies.append(copy)
        for copy in copies:
            copy.wait()


def partial_blocks(at, mine, theirs, gmine, gtheirs):
    rows = 1152
    return pl.pallas_call(
        partial_kernel,
        grid_spec=pltpu.PrefetchScalarGridSpec(
            num_scalar_prefetch=1,
            grid=(D // rows,),
            in_specs=[
                pl.BlockSpec((rows, TOK), lambda i, at: (i, 0)),
                pl.BlockSpec((rows, TOK), lambda i, at: (i, 0)),
                pl.BlockSpec((TOK, HALF), lambda i, at: (0, 0)),
                pl.BlockSpec((TOK, HALF), lambda i, at: (0, 0)),
            ],
            out_specs=[pl.BlockSpec(memory_space=pl.ANY)] * 4,
            scratch_shapes=[pltpu.VMEM((D, HALF), jnp.bfloat16), pltpu.SemaphoreType.DMA((4, 4))],
        ),
        out_shape=[jax.ShapeDtypeStruct((4, BLK, HALF), jnp.bfloat16)] * 4,
        compiler_params=pltpu.CompilerParams(vmem_limit_bytes=VMEM_LIMIT),
        cost_estimate=pl.CostEstimate(flops=4 * D * HALF * TOK, bytes_accessed=10 * 2**20, transcendentals=0),
    )(at, mine, theirs, gmine, gtheirs)


def sum_kernel(at_ref, a, b, c, d, r0, r1, r2, r3):
    total = a[0].astype(jnp.float32) + b[0].astype(jnp.float32) + c[0].astype(jnp.float32) + d[0].astype(jnp.float32)
    total = total.astype(jnp.bfloat16)
    for j, r in enumerate((r0, r1, r2, r3)):

        @pl.when(pl.program_id(0) == j)
        def _():
            r[...] = total


def sum_blocks(at, blocks):
    spec = pl.BlockSpec((1, BLK, HALF), lambda j, at: (lax.rem(at[1] + j, 4), 0, 0))
    return pl.pallas_call(
        sum_kernel,
        grid_spec=pltpu.PrefetchScalarGridSpec(
            num_scalar_prefetch=1,
            grid=(4,),
            in_specs=[spec] * 4,
            out_specs=[pl.BlockSpec((BLK, HALF), lambda j, at: (0, 0))] * 4,
        ),
        out_shape=[jax.ShapeDtypeStruct((BLK, HALF), jnp.bfloat16)] * 4,
        compiler_params=pltpu.CompilerParams(vmem_limit_bytes=VMEM_LIMIT),
        cost_estimate=pl.CostEstimate(flops=0, bytes_accessed=6 * 2**20, transcendentals=0),
    )(at, *blocks)


def product_kernel(at_ref, x_ref, g_ref, *rest):
    parts, (keys_ref, grad_ref, w, sem) = rest[:8], rest[8:]
    first, second, core = at_ref[0], at_ref[1], at_ref[2]
    copies = []
    for own in range(2):
        side = core if own == 0 else 1 - core
        ahead, behind = (first, second) if own == 0 else (second, first)
        for k in range(4):
            for j in range(4):
                f, s = lax.rem(ahead + j, 4), lax.rem(behind + k, 4)
                block = jnp.where(side == 0, 4 * s + f, 4 * f + s)
                copy = pltpu.make_async_copy(
                    parts[4 * own + k].at[j],
                    w.at[pl.ds(pl.multiple_of(block * BLK, BLK), BLK), pl.ds(pl.multiple_of(side * HALF, HALF), HALF)],
                    sem.at[own, k, j],
                )
                copy.start()
                copies.append(copy)
    for copy in copies:
        copy.wait()
    rows = 1152
    total = jnp.zeros((TOK, KD), jnp.float32)
    for i in range(D // rows):
        chunk = slice(i * rows, (i + 1) * rows)
        total += jnp.dot(x_ref[:, chunk], w[chunk, :], preferred_element_type=jnp.float32)
        grad_ref[:, chunk] = lax.dot_general(
            g_ref[...], w[chunk, :], (((1,), (1,)), ((), ())), preferred_element_type=jnp.float32
        ).astype(jnp.bfloat16)
    keys_ref[...] = total.astype(jnp.bfloat16)


def products(at, normed, key_grad, parts):
    vmem = pl.BlockSpec(memory_space=pltpu.VMEM)
    return pl.pallas_call(
        product_kernel,
        in_specs=[pl.BlockSpec(memory_space=pltpu.SMEM), vmem, vmem] + [pl.BlockSpec(memory_space=pl.ANY)] * 8,
        out_specs=[vmem, vmem],
        out_shape=[
            jax.ShapeDtypeStruct((TOK, KD), jnp.bfloat16),
            jax.ShapeDtypeStruct((TOK, D), jnp.bfloat16),
        ],
        scratch_shapes=[pltpu.VMEM((D, KD), jnp.bfloat16), pltpu.SemaphoreType.DMA((2, 4, 4))],
        compiler_params=pltpu.CompilerParams(vmem_limit_bytes=VMEM_LIMIT),
        cost_estimate=pl.CostEstimate(flops=4 * D * KD * TOK, bytes_accessed=16 * 2**20, transcendentals=0),
    )(at, normed, key_grad, *parts)


def local(normed, key_weight, key_grad):
    zl, y, x, zh, c = (lax.axis_index(name) for name in AXES)
    first, second = jnp.where(c == 0, x, y), jnp.where(c == 0, y, x)
    at = jnp.stack([first, second, c]).astype(jnp.int32)

    def half(a, which):
        return lax.dynamic_slice_in_dim(a, which * HALF, HALF, axis=1)

    w_mine, w_theirs = half(key_weight, c), half(key_weight, 1 - c)
    w_core = send(w_theirs, other_core)
    w_mirror = send(w_mine, mirror)
    w_both = send(w_theirs, lambda at: other_core(mirror(at)))
    quads = jnp.stack([w_mine, w_core, w_mirror, w_both]).reshape(2, 2, 72, HALF)
    quads = jnp.where(c == 0, quads, quads[:, ::-1])
    quads = jnp.where(zh == 0, quads, quads[::-1])
    block = quads.reshape(BLK, HALF)

    mine = quantize(normed)
    theirs = send(mine, other_core)
    g_theirs = send(half(key_grad, 1 - c), other_core)
    out = partial_blocks(at, mine, theirs, half(key_grad, c), g_theirs)

    line = jnp.stack([block] + [send(block, first_by(-j)) for j in (1, 2, 3)])
    first_sums = [out[0]] + [send(out[j], first_by(j)) for j in (1, 2, 3)]
    planes = [line] + [send(line, second_by(-j)) for j in (1, 2, 3)]
    sums = sum_blocks(at, first_sums)
    column = [sums[0]] + [send(sums[j], second_by(j)) for j in (1, 2, 3)]
    total = sum(a.astype(jnp.float32) for a in column).astype(jnp.bfloat16)

    swapped = [send(p, other_core) for p in planes]
    keys, input_grad = products(at, normed, key_grad, planes + swapped)

    units = total.reshape(2, 2, 72, 4, 128).transpose(0, 3, 1, 2, 4).reshape(16, 72, 128)
    units = lax.all_to_all(units, ("zh", "zl", "c"), 0, 0, tiled=True)
    piece = jnp.sum(units.reshape(8, 2, 72, 128).astype(jnp.float32), axis=0)
    ring = jnp.stack([piece] + [send(piece, zl_by(-j)) for j in (1, 2, 3)])
    ring = lax.dynamic_slice_in_dim(jnp.concatenate([ring, ring]), (4 - zl) % 4, 4, axis=0)
    weight_grad = ring.transpose(2, 1, 0, 3).reshape(72, KD)
    return keys, input_grad, weight_grad


def solution(mesh):
    fine = Mesh(mesh.devices.reshape(SIZES), AXES)
    fsdp = ("y", "x", "zh", "c")
    tokens, rows = P(AXES, None), P(fsdp, None)
    return jax.shard_map(
        local,
        mesh=fine,
        in_specs=(tokens, rows, tokens),
        out_specs=(tokens, tokens, rows),
        check_vma=False,
    )
```

```python
import functools

import jax
import jax.numpy as jnp
from jax import lax
from jax.experimental import pallas as pl
from jax.experimental.pallas import tpu as pltpu
from jax.sharding import Mesh, PartitionSpec as P

GROUP = 128
TAIL = 32
AXES = ("zl", "y", "x", "zh", "c")
SIZES = (4, 4, 4, 2, 2)
TOK = 256
D = 4608
KD = 1024
HALF = KD // 2
BLK = D // 16
VMEM_LIMIT = 48 * 1024 * 1024


barrier = lax.optimization_barrier


def pairs(move):
    out = []
    for i in range(256):
        rest, at = i, {}
        for name, size in zip(reversed(AXES), reversed(SIZES)):
            at[name] = rest % size
            rest //= size
        to = move(dict(at))
        j = 0
        for name, size in zip(AXES, SIZES):
            j = j * size + to[name] % size
        out.append((i, j))
    return out


def send(value, move):
    return lax.ppermute(value, AXES, pairs(move))


def other_core(at):
    at["c"] ^= 1
    return at


def mirror(at):
    at["zh"] ^= 1
    at["zl"] = 3 - at["zl"]
    return at


def first_by(step):
    def move(at):
        at["x" if at["c"] == 0 else "y"] += step
        return at

    return move


def second_by(step):
    def move(at):
        at["y" if at["c"] == 0 else "x"] += step
        return at

    return move


def z_by(step):
    def move(at):
        z = (4 * at["zh"] + at["zl"] + step) % 8
        at["zh"], at["zl"] = z // 4, z % 4
        return at

    return move


def zl_by(step):
    def move(at):
        at["zl"] += step
        return at

    return move


def restored(x):
    v = x.astype(jnp.float32).T
    scale = jnp.max(jnp.abs(v), axis=0, keepdims=True)
    low = (0.25 * scale).astype(jnp.bfloat16).astype(jnp.float32)
    high = (0.75 * scale).astype(jnp.bfloat16).astype(jnp.float32)
    twice = v + v
    mag = jnp.where((twice >= scale) | (twice < -scale), high, low)
    r = jnp.where(v >= 0.0, mag, -mag)
    token = lax.broadcasted_iota(jnp.int32, r.shape, 1)
    return jnp.where(token >= TOK - TAIL, v, r).astype(jnp.bfloat16)


def quantize_kernel(x_ref, out_ref):
    for g in range(x_ref.shape[1] // GROUP):
        span = slice(g * GROUP, (g + 1) * GROUP)
        out_ref[span, :] = restored(x_ref[:, span])


def quantize(normed):
    width = 6 * GROUP
    return pl.pallas_call(
        quantize_kernel,
        grid=(D // width,),
        in_specs=[pl.BlockSpec((TOK, width), lambda i: (0, i))],
        out_specs=pl.BlockSpec((width, TOK), lambda i: (i, 0)),
        out_shape=jax.ShapeDtypeStruct((D, TOK), jnp.bfloat16),
        compiler_params=pltpu.CompilerParams(vmem_limit_bytes=VMEM_LIMIT),
        cost_estimate=pl.CostEstimate(flops=2 * D * HALF * TOK, bytes_accessed=4 * D * TOK, transcendentals=0),
    )(normed)


ROWS = D // 4


def partial_kernel(at_ref, mine_ref, theirs_ref, gmine_ref, gtheirs_ref, o0, o1, o2, o3, acc, r, sem):
    first, core = at_ref[0], at_ref[2]
    outs = (o0, o1, o2, o3)

    def rows(block):
        return acc.at[block * BLK : (block + 1) * BLK, :]

    def make(step):
        span = slice(step * ROWS, (step + 1) * ROWS)
        total = jnp.dot(mine_ref[...], gmine_ref[...], preferred_element_type=jnp.float32)
        quantize_kernel(theirs_ref, r)
        total += jnp.dot(r[...], gtheirs_ref[...], preferred_element_type=jnp.float32)
        acc[span, :] = total.astype(jnp.bfloat16)
        for b in range(4 * step, 4 * step + 4):
            to = jnp.where(core == 0, b % 4, b // 4)
            place = jnp.where(core == 0, b // 4, b % 4)
            ahead = lax.rem(to + 4 - first, 4)
            for j, out in enumerate(outs):

                @pl.when(ahead == j)
                def _():
                    pltpu.make_async_copy(rows(b), out.at[place], sem.at[b]).start()

    for step in range(4):

        @pl.when(pl.program_id(0) == step)
        def _():
            make(step)

    @pl.when(pl.program_id(0) == 3)
    def _():
        for b in range(16):
            pltpu.make_async_copy(rows(b), o0.at[0], sem.at[b]).wait()


def partial_blocks(at, mine, theirs, gmine, gtheirs):
    acts = pl.BlockSpec((ROWS, TOK), lambda i, at: (i, 0))
    grads = pl.BlockSpec((TOK, HALF), lambda i, at: (0, 0))
    return pl.pallas_call(
        partial_kernel,
        grid_spec=pltpu.PrefetchScalarGridSpec(
            num_scalar_prefetch=1,
            grid=(4,),
            in_specs=[acts, pl.BlockSpec((TOK, ROWS), lambda i, at: (0, i)), grads, grads],
            out_specs=[pl.BlockSpec(memory_space=pl.ANY)] * 4,
            scratch_shapes=[
                pltpu.VMEM((D, HALF), jnp.bfloat16),
                pltpu.VMEM((ROWS, TOK), jnp.bfloat16),
                pltpu.SemaphoreType.DMA((16,)),
            ],
        ),
        out_shape=[jax.ShapeDtypeStruct((4, BLK, HALF), jnp.bfloat16)] * 4,
        compiler_params=pltpu.CompilerParams(vmem_limit_bytes=VMEM_LIMIT),
        cost_estimate=pl.CostEstimate(flops=3 * 4 * D * HALF * TOK, bytes_accessed=10 * 2**20, transcendentals=0),
    )(at, mine, theirs, gmine, gtheirs)


def sum_kernel(at_ref, a, b, c, d, r0, r1, r2, r3):
    total = a[0].astype(jnp.float32) + b[0].astype(jnp.float32) + c[0].astype(jnp.float32) + d[0].astype(jnp.float32)
    for j, r in enumerate((r0, r1, r2, r3)):

        @pl.when(pl.program_id(0) == j)
        def _():
            r[...] = total.astype(r.dtype)


def sum_blocks(at, blocks):
    spec = pl.BlockSpec((1, BLK, HALF), lambda j, at: (lax.rem(at[1] + j, 4), 0, 0))
    return pl.pallas_call(
        sum_kernel,
        grid_spec=pltpu.PrefetchScalarGridSpec(
            num_scalar_prefetch=1,
            grid=(4,),
            in_specs=[spec] * 4,
            out_specs=[pl.BlockSpec((BLK, HALF), lambda j, at: (0, 0))] * 4,
        ),
        out_shape=[jax.ShapeDtypeStruct((BLK, HALF), jnp.bfloat16 if j else jnp.float32) for j in range(4)],
        compiler_params=pltpu.CompilerParams(vmem_limit_bytes=VMEM_LIMIT),
        cost_estimate=pl.CostEstimate(flops=0, bytes_accessed=6 * 2**20, transcendentals=0),
    )(at, *blocks)


def units_kernel(a, b, c, d, out_ref, total):
    total[...] = a[...] + b[...].astype(jnp.float32) + c[...].astype(jnp.float32) + d[...].astype(jnp.float32)
    for zh in range(2):
        for core in range(2):
            for zl in range(4):
                s = 72 * (2 * zh + core)
                out_ref[8 * zh + 2 * zl + core] = total[s : s + 72, 128 * zl : 128 * (zl + 1)].astype(jnp.bfloat16)


def unit_sums(column):
    vmem = pl.BlockSpec(memory_space=pltpu.VMEM)
    return pl.pallas_call(
        units_kernel,
        in_specs=[vmem] * 4,
        out_specs=vmem,
        out_shape=jax.ShapeDtypeStruct((16, 72, 128), jnp.bfloat16),
        scratch_shapes=[pltpu.VMEM((BLK, HALF), jnp.float32)],
        compiler_params=pltpu.CompilerParams(vmem_limit_bytes=VMEM_LIMIT),
        cost_estimate=pl.CostEstimate(flops=0, bytes_accessed=2 * 2**20, transcendentals=0),
    )(*column)


def product_kernel(own, at_ref, x_ref, g_ref, *rest):
    line, parts, rest = rest[0], rest[1:5], rest[5:]
    if own:
        keys_ref, grad_ref, w, total, sem = rest
    else:
        half_ref, before_ref, keys_ref, grad_ref, w, total, sem = rest
    step, core = pl.program_id(0), at_ref[2]
    first, second = (at_ref[0], at_ref[1]) if own else (at_ref[1], at_ref[0])
    side = core if own else 1 - core
    turn = 2 * lax.rem(at_ref[3], 2)
    now = lax.rem(jnp.where(side == 0, second, first + turn) + step, 4)

    def copy(source, f, s, i, m):
        f, s = lax.rem(first + f, 4), lax.rem(second + s, 4)
        block = jnp.where(side == 0, 4 * s + f, 4 * f + s)
        return pltpu.make_async_copy(
            source, w.at[pl.ds(pl.multiple_of(block * BLK, BLK), BLK), :], sem.at[i, m]
        )

    @pl.when(step == 0)
    def _():
        total[...] = jnp.zeros_like(total)

        @pl.when(side == 0)
        def _():
            for m in range(4):
                copy(line.at[m], m, 0, 0, m).start()
            for i in range(1, 4):
                for m in range(4):
                    copy(parts[m].at[i - 1], turn + m, i, i, m).start()

        @pl.when(side != 0)
        def _():
            for i in range(4):
                copy(line.at[lax.rem(turn + i, 4)], turn + i, 0, i, 0).start()
                for m in range(1, 4):
                    copy(parts[i].at[m - 1], turn + i, m, i, m).start()

    for m in range(4):
        copy(line.at[0], 0, 0, step, m).wait()

    part = w[pl.ds(pl.multiple_of(now * ROWS, ROWS), ROWS), :]
    total[...] += jnp.dot(x_ref[...], part, preferred_element_type=jnp.float32)
    grad = lax.dot_general(part, g_ref[...], (((1,), (1,)), ((), ())), preferred_element_type=jnp.float32)
    if own:
        grad_ref[...] = grad
    else:
        grad_ref[...] = (grad + before_ref[...]).T.astype(grad_ref.dtype)

    @pl.when(step == 3)
    def _():
        keys = total[...].astype(jnp.bfloat16)
        if own:
            keys_ref[...] = keys
        else:

            @pl.when(core == 0)
            def _():
                keys_ref[:, :HALF] = half_ref[...]
                keys_ref[:, HALF:] = keys

            @pl.when(core != 0)
            def _():
                keys_ref[:, HALF:] = half_ref[...]
                keys_ref[:, :HALF] = keys


def products(at, normed, key_grad, parts, before=()):
    own = not before
    width = HALF if own else KD

    def now(i, at):
        side = at[2] if own else 1 - at[2]
        first, second = (at[0], at[1]) if own else (at[1], at[0])
        start = jnp.where(side == 0, second, first + 2 * lax.rem(at[3], 2))
        return lax.rem(start + i, 4)

    whole = lambda i, at: (0, 0)
    across, down = (lambda i, at: (0, now(i, at))), (lambda i, at: (now(i, at), 0))
    return pl.pallas_call(
        functools.partial(product_kernel, own),
        grid_spec=pltpu.PrefetchScalarGridSpec(
            num_scalar_prefetch=1,
            grid=(4,),
            in_specs=[pl.BlockSpec((TOK, ROWS), across), pl.BlockSpec((TOK, HALF), whole)]
            + [pl.BlockSpec(memory_space=pl.ANY)] * 5
            + ([] if own else [pl.BlockSpec((TOK, HALF), whole), pl.BlockSpec((ROWS, TOK), down)]),
            out_specs=[
                pl.BlockSpec((TOK, width), whole),
                pl.BlockSpec((ROWS, TOK), down) if own else pl.BlockSpec((TOK, ROWS), across),
            ],
            scratch_shapes=[
                pltpu.VMEM((D, HALF), jnp.bfloat16),
                pltpu.VMEM((TOK, HALF), jnp.float32),
                pltpu.SemaphoreType.DMA((4, 4)),
            ],
        ),
        out_shape=[
            jax.ShapeDtypeStruct((TOK, width), jnp.bfloat16),
            jax.ShapeDtypeStruct((D, TOK) if own else (TOK, D), jnp.float32 if own else jnp.bfloat16),
        ],
        compiler_params=pltpu.CompilerParams(vmem_limit_bytes=VMEM_LIMIT),
        cost_estimate=pl.CostEstimate(flops=2 * D * KD * TOK, bytes_accessed=12 * 2**20, transcendentals=0),
    )(at, normed, key_grad, *parts, *before)


def local(normed, key_weight, key_grad):
    zl, y, x, zh, c = (lax.axis_index(name) for name in AXES)
    first, second = jnp.where(c == 0, x, y), jnp.where(c == 0, y, x)
    at = jnp.stack([first, second, c, zl]).astype(jnp.int32)

    def half(a, which):
        return lax.dynamic_slice_in_dim(a, which * HALF, HALF, axis=1)

    w_mine, w_theirs = half(key_weight, c), half(key_weight, 1 - c)
    g_mine, g_other = half(key_grad, c), half(key_grad, 1 - c)
    x_theirs = send(normed, other_core)
    g_theirs = send(g_other, other_core)
    w_core = send(w_theirs, other_core)
    w_mirror = send(w_mine, mirror)
    w_both = send(w_theirs, lambda at: other_core(mirror(at)))
    mine = quantize(normed)
    w_core, w_mirror, w_both, mine = barrier((w_core, w_mirror, w_both, mine))
    quads = jnp.stack([w_mine, w_core, w_mirror, w_both]).reshape(2, 2, 72, HALF)
    quads = jnp.where(c == 0, quads, quads[:, ::-1])
    quads = jnp.where(zh == 0, quads, quads[::-1])
    block = quads.reshape(BLK, HALF)
    x_theirs, block, mine = barrier((x_theirs, block, mine))
    near = [send(block, first_by(-j)) for j in (1, 2, 3)]

    out = partial_blocks(at, mine, x_theirs, g_mine, g_theirs)
    out, near = barrier((out, near))

    line = jnp.stack([block] + near)
    some = lax.dynamic_slice_in_dim(line, 2 * (zl % 2), 2, axis=0)
    far = [send(some, second_by(-j)) for j in (1, 2, 3)]
    out = list(out)
    out[2], far[1] = barrier((out[2], far[1]))
    got2, got1, got3 = (send(out[j], first_by(j)) for j in (2, 1, 3))
    far_a, far_b = jnp.stack([f[0] for f in far]), jnp.stack([f[1] for f in far])
    parts = [far_a, far_b, send(far_a, z_by(-1)), send(far_b, z_by(1))]

    sums = sum_blocks(at, [out[0], got1, got2, got3])
    column = [sums[0]] + [send(sums[j], second_by(j)) for j in (1, 2, 3)]
    units = unit_sums(column)
    units, line, parts = barrier((units, line, parts))
    swapped = [send(p, other_core) for p in [line] + parts]
    keys_mine, grad = products(at, normed, g_mine, [line] + parts)
    units = lax.all_to_all(units, ("zh", "zl", "c"), 0, 0, tiled=True)
    units, keys_mine, grad, swapped = barrier((units, keys_mine, grad, swapped))
    piece = jnp.sum(units.reshape(8, 2, 72, 128).astype(jnp.float32), axis=0)
    piece, swapped = barrier((piece, swapped))
    ring = jnp.stack([piece] + [send(piece, zl_by(-j)) for j in (1, 2, 3)])
    ring = lax.dynamic_slice_in_dim(jnp.concatenate([ring, ring]), (4 - zl) % 4, 4, axis=0)
    weight_grad = ring.transpose(2, 1, 0, 3).reshape(72, KD)
    keys, input_grad = products(at, normed, g_other, swapped, (keys_mine, grad))
    return keys, input_grad, weight_grad


def solution(mesh):
    fine = Mesh(mesh.devices.reshape(SIZES), AXES)
    fsdp = ("y", "x", "zh", "c")
    tokens, rows = P(AXES, None), P(fsdp, None)
    return jax.shard_map(
        local,
        mesh=fine,
        in_specs=(tokens, rows, tokens),
        out_specs=(tokens, tokens, rows),
        check_vma=False,
    )
```

```python
import jax
import jax.numpy as jnp
from jax import lax
from jax.experimental import pallas as pl
from jax.experimental.pallas import tpu as pltpu
from jax.sharding import Mesh, PartitionSpec as P

GROUP = 128
TAIL = 32
AXES = ("zl", "y", "x", "zh", "c")
SIZES = (4, 4, 4, 2, 2)
TOK = 256
D = 4608
KD = 1024
HALF = KD // 2
BLK = D // 16
VMEM_LIMIT = 28 * 1024 * 1024
SMALL_LIMIT = 20 * 1024 * 1024


barrier = lax.optimization_barrier


def in_hbm(x):
    return pltpu.with_memory_space_constraint(x, pltpu.HBM)


def pairs(move):
    out = []
    for i in range(256):
        rest, at = i, {}
        for name, size in zip(reversed(AXES), reversed(SIZES)):
            at[name] = rest % size
            rest //= size
        to = move(dict(at))
        j = 0
        for name, size in zip(AXES, SIZES):
            j = j * size + to[name] % size
        out.append((i, j))
    return out


def send(value, move):
    return lax.ppermute(value, AXES, pairs(move))


def other_core(at):
    at["c"] ^= 1
    return at


def mirror(at):
    at["zh"] ^= 1
    at["zl"] = 3 - at["zl"]
    return at


def first_by(step):
    def move(at):
        at["x" if at["c"] == 0 else "y"] += step
        return at

    return move


def second_by(step):
    def move(at):
        at["y" if at["c"] == 0 else "x"] += step
        return at

    return move


def z_by(step):
    def move(at):
        z = (4 * at["zh"] + at["zl"] + step) % 8
        at["zh"], at["zl"] = z // 4, z % 4
        return at

    return move


def zl_by(step):
    def move(at):
        at["zl"] += step
        return at

    return move


def restored(x):
    v = x.astype(jnp.float32).T
    scale = jnp.max(jnp.abs(v), axis=0, keepdims=True)
    low = (0.25 * scale).astype(jnp.bfloat16).astype(jnp.float32)
    high = (0.75 * scale).astype(jnp.bfloat16).astype(jnp.float32)
    twice = v + v
    mag = jnp.where((twice >= scale) | (twice < -scale), high, low)
    r = jnp.where(v >= 0.0, mag, -mag)
    token = lax.broadcasted_iota(jnp.int32, r.shape, 1)
    return jnp.where(token >= TOK - TAIL, v, r).astype(jnp.bfloat16)


def quantize_kernel(x_ref, out_ref):
    for g in range(x_ref.shape[1] // GROUP):
        span = slice(g * GROUP, (g + 1) * GROUP)
        out_ref[span, :] = restored(x_ref[:, span])


def quantize(normed):
    width = 6 * GROUP
    return pl.pallas_call(
        quantize_kernel,
        grid=(D // width,),
        in_specs=[pl.BlockSpec((TOK, width), lambda i: (0, i))],
        out_specs=pl.BlockSpec((width, TOK), lambda i: (i, 0)),
        out_shape=jax.ShapeDtypeStruct((D, TOK), jnp.bfloat16),
        compiler_params=pltpu.CompilerParams(vmem_limit_bytes=SMALL_LIMIT),
        cost_estimate=pl.CostEstimate(flops=2 * D * HALF * TOK, bytes_accessed=4 * D * TOK, transcendentals=0),
    )(normed)


ROWS = D // 4


def partial_kernel(at_ref, mine_ref, theirs_ref, gmine_ref, gtheirs_ref, o0, o1, o2, o3, acc, r, sem):
    first, core = at_ref[0], at_ref[2]
    outs = (o0, o1, o2, o3)

    def rows(block):
        return acc.at[block * BLK : (block + 1) * BLK, :]

    def make(step):
        span = slice(step * ROWS, (step + 1) * ROWS)
        total = jnp.dot(mine_ref[...], gmine_ref[...], preferred_element_type=jnp.float32)
        quantize_kernel(theirs_ref, r)
        total += jnp.dot(r[...], gtheirs_ref[...], preferred_element_type=jnp.float32)
        acc[span, :] = total.astype(jnp.bfloat16)
        for b in range(4 * step, 4 * step + 4):
            to = jnp.where(core == 0, b % 4, b // 4)
            place = jnp.where(core == 0, b // 4, b % 4)
            ahead = lax.rem(to + 4 - first, 4)
            for j, out in enumerate(outs):

                @pl.when(ahead == j)
                def _():
                    pltpu.make_async_copy(rows(b), out.at[place], sem.at[b]).start()

    for step in range(4):

        @pl.when(pl.program_id(0) == step)
        def _():
            make(step)

    @pl.when(pl.program_id(0) == 3)
    def _():
        for b in range(16):
            pltpu.make_async_copy(rows(b), o0.at[0], sem.at[b]).wait()


def partial_blocks(at, mine, theirs, gmine, gtheirs):
    acts = pl.BlockSpec((ROWS, TOK), lambda i, at: (i, 0))
    grads = pl.BlockSpec((TOK, HALF), lambda i, at: (0, 0))
    return pl.pallas_call(
        partial_kernel,
        grid_spec=pltpu.PrefetchScalarGridSpec(
            num_scalar_prefetch=1,
            grid=(4,),
            in_specs=[acts, pl.BlockSpec((TOK, ROWS), lambda i, at: (0, i)), grads, grads],
            out_specs=[pl.BlockSpec(memory_space=pl.ANY)] * 4,
            scratch_shapes=[
                pltpu.VMEM((D, HALF), jnp.bfloat16),
                pltpu.VMEM((ROWS, TOK), jnp.bfloat16),
                pltpu.SemaphoreType.DMA((16,)),
            ],
        ),
        out_shape=[jax.ShapeDtypeStruct((4, BLK, HALF), jnp.bfloat16)] * 4,
        compiler_params=pltpu.CompilerParams(vmem_limit_bytes=SMALL_LIMIT),
        cost_estimate=pl.CostEstimate(flops=3 * 4 * D * HALF * TOK, bytes_accessed=10 * 2**20, transcendentals=0),
    )(at, mine, theirs, gmine, gtheirs)


def sum_kernel(at_ref, a, b, c, d, r0, r1, r2, r3):
    total = a[0].astype(jnp.float32) + b[0].astype(jnp.float32) + c[0].astype(jnp.float32) + d[0].astype(jnp.float32)
    for j, r in enumerate((r0, r1, r2, r3)):

        @pl.when(pl.program_id(0) == j)
        def _():
            r[...] = total.astype(r.dtype)


def sum_blocks(at, blocks):
    spec = pl.BlockSpec((1, BLK, HALF), lambda j, at: (lax.rem(at[1] + j, 4), 0, 0))
    return pl.pallas_call(
        sum_kernel,
        grid_spec=pltpu.PrefetchScalarGridSpec(
            num_scalar_prefetch=1,
            grid=(4,),
            in_specs=[spec] * 4,
            out_specs=[pl.BlockSpec((BLK, HALF), lambda j, at: (0, 0))] * 4,
        ),
        out_shape=[jax.ShapeDtypeStruct((BLK, HALF), jnp.bfloat16 if j else jnp.float32) for j in range(4)],
        compiler_params=pltpu.CompilerParams(vmem_limit_bytes=SMALL_LIMIT),
        cost_estimate=pl.CostEstimate(flops=0, bytes_accessed=6 * 2**20, transcendentals=0),
    )(at, *blocks)


def units_kernel(a, b, c, d, out_ref, total):
    total[...] = a[...] + b[...].astype(jnp.float32) + c[...].astype(jnp.float32) + d[...].astype(jnp.float32)
    for zh in range(2):
        for core in range(2):
            for zl in range(4):
                s = 72 * (2 * zh + core)
                out_ref[8 * zh + 2 * zl + core] = total[s : s + 72, 128 * zl : 128 * (zl + 1)].astype(jnp.bfloat16)


def unit_sums(column):
    vmem = pl.BlockSpec(memory_space=pltpu.VMEM)
    return pl.pallas_call(
        units_kernel,
        in_specs=[vmem] * 4,
        out_specs=vmem,
        out_shape=jax.ShapeDtypeStruct((16, 72, 128), jnp.bfloat16),
        scratch_shapes=[pltpu.VMEM((BLK, HALF), jnp.float32)],
        compiler_params=pltpu.CompilerParams(vmem_limit_bytes=SMALL_LIMIT),
        cost_estimate=pl.CostEstimate(flops=0, bytes_accessed=2 * 2**20, transcendentals=0),
    )(*column)


def product_kernel(at_ref, x_ref, g_ref, *rest):
    sides, (keys_ref, grad_ref, w, total, sem) = (rest[:5], rest[5:10]), rest[10:]
    step, core = pl.program_id(0), at_ref[2]
    x_at, y_at = jnp.where(core == 0, at_ref[0], at_ref[1]), jnp.where(core == 0, at_ref[1], at_ref[0])
    turn = 2 * lax.rem(at_ref[3], 2)

    def copy(source, y, x, side, i, m):
        y, x = lax.rem(y_at + y, 4), lax.rem(x_at + x, 4)
        rows = pl.ds(pl.multiple_of((4 * y + x) * BLK, BLK), BLK)
        columns = slice(side * HALF, (side + 1) * HALF)
        return pltpu.make_async_copy(source, w.at[rows, columns], sem.at[side, i, m])

    def start(side, line, parts, i):
        ahead = lax.rem(turn + i, 4)
        if side == 1:
            copy(line.at[ahead], ahead, 0, side, i, 0).start()
            for m in range(1, 4):
                copy(parts[i].at[m - 1], ahead, m, side, i, m).start()
            return

        @pl.when(ahead == 0)
        def _():
            for m in range(4):
                copy(line.at[m], 0, m, side, i, m).start()

        @pl.when(ahead != 0)
        def _():
            for m in range(4):
                copy(parts[m].at[jnp.maximum(ahead - 1, 0)], ahead, turn + m, side, i, m).start()

    for i in range(4):
        for own in range(2):

            @pl.when((step == max(i - 1, 0)) & (core == own))
            def _():
                for side in range(2):
                    mine = sides[0 if side == own else 1]
                    start(side, mine[0], mine[1:], i)

    @pl.when(step == 0)
    def _():
        total[...] = jnp.zeros_like(total)

    for side in range(2):
        for m in range(4):
            copy(sides[0][0].at[0], 0, 0, side, step, m).wait()

    now = lax.rem(y_at + turn + step, 4)
    part = w[pl.ds(pl.multiple_of(now * ROWS, ROWS), ROWS), :]
    total[...] += jnp.dot(x_ref[...], part, preferred_element_type=jnp.float32)
    grad = lax.dot_general(g_ref[...], part, (((1,), (1,)), ((), ())), preferred_element_type=jnp.float32)
    grad_ref[...] = grad.astype(grad_ref.dtype)

    @pl.when(step == pl.num_programs(0) - 1)
    def _():
        keys_ref[...] = total[...].astype(jnp.bfloat16)


def products(at, normed, key_grad, parts, swapped):
    def across(i, at):
        y = jnp.where(at[2] == 0, at[1], at[0])
        return (0, lax.rem(y + 2 * lax.rem(at[3], 2) + i, 4))

    whole = lambda i, at: (0, 0)
    return pl.pallas_call(
        product_kernel,
        grid_spec=pltpu.PrefetchScalarGridSpec(
            num_scalar_prefetch=1,
            grid=(4,),
            in_specs=[pl.BlockSpec((TOK, ROWS), across), pl.BlockSpec((TOK, KD), whole)]
            + [pl.BlockSpec(memory_space=pl.ANY)] * 10,
            out_specs=[pl.BlockSpec((TOK, KD), whole), pl.BlockSpec((TOK, ROWS), across)],
            scratch_shapes=[
                pltpu.VMEM((D, KD), jnp.bfloat16),
                pltpu.VMEM((TOK, KD), jnp.float32),
                pltpu.SemaphoreType.DMA((2, 4, 4)),
            ],
        ),
        out_shape=[jax.ShapeDtypeStruct((TOK, KD), jnp.bfloat16), jax.ShapeDtypeStruct((TOK, D), jnp.bfloat16)],
        compiler_params=pltpu.CompilerParams(vmem_limit_bytes=VMEM_LIMIT),
        cost_estimate=pl.CostEstimate(flops=4 * D * KD * TOK, bytes_accessed=14 * 2**20, transcendentals=0),
    )(at, in_hbm(normed), in_hbm(key_grad), *parts, *swapped)


def local(normed, key_weight, key_grad):
    zl, y, x, zh, c = (lax.axis_index(name) for name in AXES)
    first, second = jnp.where(c == 0, x, y), jnp.where(c == 0, y, x)
    at = jnp.stack([first, second, c, zl]).astype(jnp.int32)

    def half(a, which):
        return lax.dynamic_slice_in_dim(a, which * HALF, HALF, axis=1)

    w_mine, w_theirs = half(key_weight, c), half(key_weight, 1 - c)
    g_mine, g_other = half(key_grad, c), half(key_grad, 1 - c)
    x_theirs = send(normed, other_core)
    g_theirs = send(g_other, other_core)
    w_core = send(w_theirs, other_core)
    w_mirror = send(w_mine, mirror)
    w_both = send(w_theirs, lambda at: other_core(mirror(at)))
    mine = quantize(normed)
    w_core, w_mirror, w_both, mine = barrier((w_core, w_mirror, w_both, mine))
    quads = jnp.stack([w_mine, w_core, w_mirror, w_both]).reshape(2, 2, 72, HALF)
    quads = jnp.where(c == 0, quads, quads[:, ::-1])
    quads = jnp.where(zh == 0, quads, quads[::-1])
    block = quads.reshape(BLK, HALF)
    x_theirs, block, mine = barrier((x_theirs, block, mine))
    near = [send(block, first_by(-j)) for j in (1, 2, 3)]

    out = partial_blocks(at, mine, x_theirs, g_mine, g_theirs)
    out, near = barrier((out, near))

    line = jnp.stack([block] + near)
    some = jnp.where(zl % 2 == 0, jnp.stack([block, near[0]]), jnp.stack(near[1:]))
    far = [send(some, second_by(-j)) for j in (1, 2, 3)]
    out = list(out)
    out[2], far[1] = barrier((out[2], far[1]))
    got2, got1, got3 = (send(out[j], first_by(j)) for j in (2, 1, 3))
    far_a, far_b = jnp.stack([f[0] for f in far]), jnp.stack([f[1] for f in far])
    parts = [far_a, far_b, send(far_a, z_by(-1)), send(far_b, z_by(1))]

    sums = sum_blocks(at, [out[0], got1, got2, got3])
    column = [sums[0]] + [send(sums[j], second_by(j)) for j in (1, 2, 3)]
    units = unit_sums(column)
    units, line, parts = barrier((units, line, parts))
    swapped = [send(p, other_core) for p in [line] + parts]
    keys, input_grad = products(at, normed, key_grad, [line] + parts, swapped)
    units = lax.all_to_all(units, ("zh", "zl", "c"), 0, 0, tiled=True)
    units, keys, input_grad = barrier((units, keys, input_grad))
    piece = jnp.sum(units.reshape(8, 2, 72, 128).astype(jnp.float32), axis=0)
    ring = jnp.stack([piece] + [send(piece, zl_by(-j)) for j in (1, 2, 3)])
    ring = lax.dynamic_slice_in_dim(jnp.concatenate([ring, ring]), (4 - zl) % 4, 4, axis=0)
    weight_grad = ring.transpose(2, 1, 0, 3).reshape(72, KD)
    return keys, input_grad, weight_grad


def solution(mesh):
    fine = Mesh(mesh.devices.reshape(SIZES), AXES)
    fsdp = ("y", "x", "zh", "c")
    tokens, rows = P(AXES, None), P(fsdp, None)
    return jax.shard_map(
        local,
        mesh=fine,
        in_specs=(tokens, rows, tokens),
        out_specs=(tokens, tokens, rows),
        check_vma=False,
    )
```

```python
import jax
import jax.numpy as jnp
from jax import lax
from jax.experimental import pallas as pl
from jax.experimental.pallas import tpu as pltpu
from jax.sharding import Mesh, PartitionSpec as P

GROUP = 128
TAIL = 32
AXES = ("zl", "y", "x", "zh", "c")
SIZES = (4, 4, 4, 2, 2)
TOK = 256
D = 4608
KD = 1024
HALF = KD // 2
BLK = D // 16
VMEM_LIMIT = 28 * 1024 * 1024
SMALL_LIMIT = 20 * 1024 * 1024


barrier = lax.optimization_barrier


def in_hbm(x):
    return pltpu.with_memory_space_constraint(x, pltpu.HBM)


def pairs(move):
    out = []
    for i in range(256):
        rest, at = i, {}
        for name, size in zip(reversed(AXES), reversed(SIZES)):
            at[name] = rest % size
            rest //= size
        to = move(dict(at))
        j = 0
        for name, size in zip(AXES, SIZES):
            j = j * size + to[name] % size
        out.append((i, j))
    return out


def send(value, move):
    return lax.ppermute(value, AXES, pairs(move))


def other_core(at):
    at["c"] ^= 1
    return at


def mirror(at):
    at["zh"] ^= 1
    at["zl"] = 3 - at["zl"]
    return at


def first_by(step):
    def move(at):
        at["x" if at["c"] == 0 else "y"] += step
        return at

    return move


def second_by(step):
    def move(at):
        at["y" if at["c"] == 0 else "x"] += step
        return at

    return move


def z_by(step):
    def move(at):
        z = (4 * at["zh"] + at["zl"] + step) % 8
        at["zh"], at["zl"] = z // 4, z % 4
        return at

    return move


def zl_by(step):
    def move(at):
        at["zl"] += step
        return at

    return move


def restored(x):
    v = x.astype(jnp.float32).T
    scale = jnp.max(jnp.abs(v), axis=0, keepdims=True)
    low = (0.25 * scale).astype(jnp.bfloat16).astype(jnp.float32)
    high = (0.75 * scale).astype(jnp.bfloat16).astype(jnp.float32)
    twice = v + v
    mag = jnp.where((twice >= scale) | (twice < -scale), high, low)
    r = jnp.where(v >= 0.0, mag, -mag)
    token = lax.broadcasted_iota(jnp.int32, r.shape, 1)
    return jnp.where(token >= TOK - TAIL, v, r).astype(jnp.bfloat16)


def quantize_kernel(x_ref, out_ref):
    for g in range(x_ref.shape[1] // GROUP):
        span = slice(g * GROUP, (g + 1) * GROUP)
        out_ref[span, :] = restored(x_ref[:, span])


def quantize(normed):
    width = 6 * GROUP
    return pl.pallas_call(
        quantize_kernel,
        grid=(D // width,),
        in_specs=[pl.BlockSpec((TOK, width), lambda i: (0, i))],
        out_specs=pl.BlockSpec((width, TOK), lambda i: (i, 0)),
        out_shape=jax.ShapeDtypeStruct((D, TOK), jnp.bfloat16),
        compiler_params=pltpu.CompilerParams(vmem_limit_bytes=SMALL_LIMIT),
        cost_estimate=pl.CostEstimate(flops=2 * D * HALF * TOK, bytes_accessed=4 * D * TOK, transcendentals=0),
    )(normed)


ROWS = D // 4


def partial_kernel(at_ref, mine_ref, theirs_ref, gmine_ref, gtheirs_ref, o0, o1, o2, o3, acc, r, sem):
    first, core = at_ref[0], at_ref[2]
    outs = (o0, o1, o2, o3)

    def rows(block):
        return acc.at[block * BLK : (block + 1) * BLK, :]

    def make(step):
        span = slice(step * ROWS, (step + 1) * ROWS)
        total = jnp.dot(mine_ref[...], gmine_ref[...], preferred_element_type=jnp.float32)
        quantize_kernel(theirs_ref, r)
        total += jnp.dot(r[...], gtheirs_ref[...], preferred_element_type=jnp.float32)
        acc[span, :] = total.astype(jnp.bfloat16)
        for b in range(4 * step, 4 * step + 4):
            to = jnp.where(core == 0, b % 4, b // 4)
            place = jnp.where(core == 0, b // 4, b % 4)
            ahead = lax.rem(to + 4 - first, 4)
            for j, out in enumerate(outs):

                @pl.when(ahead == j)
                def _():
                    pltpu.make_async_copy(rows(b), out.at[place], sem.at[b]).start()

    for step in range(4):

        @pl.when(pl.program_id(0) == step)
        def _():
            make(step)

    @pl.when(pl.program_id(0) == 3)
    def _():
        for b in range(16):
            pltpu.make_async_copy(rows(b), o0.at[0], sem.at[b]).wait()


def partial_blocks(at, mine, theirs, gmine, gtheirs):
    acts = pl.BlockSpec((ROWS, TOK), lambda i, at: (i, 0))
    grads = pl.BlockSpec((TOK, HALF), lambda i, at: (0, 0))
    return pl.pallas_call(
        partial_kernel,
        grid_spec=pltpu.PrefetchScalarGridSpec(
            num_scalar_prefetch=1,
            grid=(4,),
            in_specs=[acts, pl.BlockSpec((TOK, ROWS), lambda i, at: (0, i)), grads, grads],
            out_specs=[pl.BlockSpec(memory_space=pl.ANY)] * 4,
            scratch_shapes=[
                pltpu.VMEM((D, HALF), jnp.bfloat16),
                pltpu.VMEM((ROWS, TOK), jnp.bfloat16),
                pltpu.SemaphoreType.DMA((16,)),
            ],
        ),
        out_shape=[jax.ShapeDtypeStruct((4, BLK, HALF), jnp.bfloat16)] * 4,
        compiler_params=pltpu.CompilerParams(vmem_limit_bytes=SMALL_LIMIT),
        cost_estimate=pl.CostEstimate(flops=3 * 4 * D * HALF * TOK, bytes_accessed=10 * 2**20, transcendentals=0),
    )(at, mine, theirs, gmine, gtheirs)


def sum_kernel(at_ref, a, b, c, d, r0, r1, r2, r3):
    total = a[0].astype(jnp.float32) + b[0].astype(jnp.float32) + c[0].astype(jnp.float32) + d[0].astype(jnp.float32)
    for j, r in enumerate((r0, r1, r2, r3)):

        @pl.when(pl.program_id(0) == j)
        def _():
            r[...] = total.astype(r.dtype)


def sum_blocks(at, blocks):
    spec = pl.BlockSpec((1, BLK, HALF), lambda j, at: (lax.rem(at[1] + j, 4), 0, 0))
    return pl.pallas_call(
        sum_kernel,
        grid_spec=pltpu.PrefetchScalarGridSpec(
            num_scalar_prefetch=1,
            grid=(4,),
            in_specs=[spec] * 4,
            out_specs=[pl.BlockSpec((BLK, HALF), lambda j, at: (0, 0))] * 4,
        ),
        out_shape=[jax.ShapeDtypeStruct((BLK, HALF), jnp.bfloat16 if j else jnp.float32) for j in range(4)],
        compiler_params=pltpu.CompilerParams(vmem_limit_bytes=SMALL_LIMIT),
        cost_estimate=pl.CostEstimate(flops=0, bytes_accessed=6 * 2**20, transcendentals=0),
    )(at, *blocks)


def units_kernel(a, b, c, d, out_ref, total):
    total[...] = a[...] + b[...].astype(jnp.float32) + c[...].astype(jnp.float32) + d[...].astype(jnp.float32)
    for zh in range(2):
        for core in range(2):
            for zl in range(4):
                s = 72 * (2 * zh + core)
                out_ref[8 * zh + 2 * zl + core] = total[s : s + 72, 128 * zl : 128 * (zl + 1)].astype(jnp.bfloat16)


def unit_sums(column):
    vmem = pl.BlockSpec(memory_space=pltpu.VMEM)
    return pl.pallas_call(
        units_kernel,
        in_specs=[vmem] * 4,
        out_specs=vmem,
        out_shape=jax.ShapeDtypeStruct((16, 72, 128), jnp.bfloat16),
        scratch_shapes=[pltpu.VMEM((BLK, HALF), jnp.float32)],
        compiler_params=pltpu.CompilerParams(vmem_limit_bytes=SMALL_LIMIT),
        cost_estimate=pl.CostEstimate(flops=0, bytes_accessed=2 * 2**20, transcendentals=0),
    )(*column)


def product_kernel(at_ref, x_ref, g_ref, *rest):
    sides, (keys_ref, grad_ref, w, x, g, total, sem, x_sem, g_sem) = (rest[:5], rest[5:10]), rest[10:]
    step, core = pl.program_id(0), at_ref[2]
    x_at, y_at = jnp.where(core == 0, at_ref[0], at_ref[1]), jnp.where(core == 0, at_ref[1], at_ref[0])
    turn = 2 * (at_ref[3] & 1)

    def quarter(i):
        return pl.ds(pl.multiple_of(((y_at + turn + i) & 3) * ROWS, ROWS), ROWS)

    def fetch(i):
        return pltpu.make_async_copy(x_ref.at[:, quarter(i)], x.at[:, quarter(i)], x_sem.at[i])

    def copy(source, dy, dx, side, i):
        block = 4 * ((y_at + dy) & 3) + ((x_at + dx) & 3)
        rows = pl.ds(pl.multiple_of(block * BLK, BLK), BLK)
        columns = slice(side * HALF, (side + 1) * HALF)
        return pltpu.make_async_copy(source, w.at[rows, columns], sem.at[side, i])

    def start(side, line, parts, i):
        ahead = (turn + i) & 3
        if side == 1:
            copy(line.at[ahead], ahead, 0, side, i).start()
            for m in range(1, 4):
                copy(parts[i].at[m - 1], ahead, m, side, i).start()
            return

        @pl.when(ahead == 0)
        def _():
            for m in range(4):
                copy(line.at[m], 0, m, side, i).start()

        @pl.when(ahead != 0)
        def _():
            for m in range(4):
                copy(parts[m].at[jnp.maximum(ahead - 1, 0)], ahead, turn + m, side, i).start()

    @pl.when(step == 0)
    def _():
        pltpu.make_async_copy(g_ref, g, g_sem).start()
        for own in range(2):

            @pl.when(core == own)
            def _():
                for i in range(4):
                    fetch(i).start()
                    for side in range(2):
                        mine = sides[0 if side == own else 1]
                        start(side, mine[0], mine[1:], i)

        total[...] = jnp.zeros_like(total)
        pltpu.make_async_copy(g_ref, g, g_sem).wait()

    fetch(step).wait()
    rows = quarter(step)
    for side in range(2):
        part = w.at[rows, side * HALF : (side + 1) * HALF]
        pltpu.make_async_copy(part, part, sem.at[side, step]).wait()
    part = w[rows, :]
    total[...] += jnp.dot(x[:, rows], part, preferred_element_type=jnp.float32)
    grad = lax.dot_general(g[...], part, (((1,), (1,)), ((), ())), preferred_element_type=jnp.float32)
    grad_ref[...] = grad.astype(grad_ref.dtype)

    @pl.when(step == pl.num_programs(0) - 1)
    def _():
        keys_ref[...] = total[...].astype(jnp.bfloat16)


def products(at, normed, key_grad, parts, swapped):
    def across(i, at):
        y = jnp.where(at[2] == 0, at[1], at[0])
        return (0, lax.rem(y + 2 * lax.rem(at[3], 2) + i, 4))

    whole = lambda i, at: (0, 0)
    return pl.pallas_call(
        product_kernel,
        grid_spec=pltpu.PrefetchScalarGridSpec(
            num_scalar_prefetch=1,
            grid=(4,),
            in_specs=[pl.BlockSpec(memory_space=pl.ANY)] * 12,
            out_specs=[pl.BlockSpec((TOK, KD), whole), pl.BlockSpec((TOK, ROWS), across)],
            scratch_shapes=[
                pltpu.VMEM((D, KD), jnp.bfloat16),
                pltpu.VMEM((TOK, D), jnp.bfloat16),
                pltpu.VMEM((TOK, KD), jnp.bfloat16),
                pltpu.VMEM((TOK, KD), jnp.float32),
                pltpu.SemaphoreType.DMA((2, 4)),
                pltpu.SemaphoreType.DMA((4,)),
                pltpu.SemaphoreType.DMA,
            ],
        ),
        out_shape=[jax.ShapeDtypeStruct((TOK, KD), jnp.bfloat16), jax.ShapeDtypeStruct((TOK, D), jnp.bfloat16)],
        compiler_params=pltpu.CompilerParams(vmem_limit_bytes=VMEM_LIMIT),
        cost_estimate=pl.CostEstimate(flops=4 * D * KD * TOK, bytes_accessed=14 * 2**20, transcendentals=0),
    )(at, in_hbm(normed), in_hbm(key_grad), *parts, *swapped)


def local(normed, key_weight, key_grad):
    zl, y, x, zh, c = (lax.axis_index(name) for name in AXES)
    first, second = jnp.where(c == 0, x, y), jnp.where(c == 0, y, x)
    at = jnp.stack([first, second, c, zl]).astype(jnp.int32)

    def half(a, which):
        return lax.dynamic_slice_in_dim(a, which * HALF, HALF, axis=1)

    w_mine, w_theirs = half(key_weight, c), half(key_weight, 1 - c)
    g_mine, g_other = half(key_grad, c), half(key_grad, 1 - c)
    x_theirs = send(normed, other_core)
    g_theirs = send(g_other, other_core)
    w_core = send(w_theirs, other_core)
    w_mirror = send(w_mine, mirror)
    w_both = send(w_theirs, lambda at: other_core(mirror(at)))
    mine = quantize(normed)
    w_core, w_mirror, w_both, mine = barrier((w_core, w_mirror, w_both, mine))
    quads = jnp.stack([w_mine, w_core, w_mirror, w_both]).reshape(2, 2, 72, HALF)
    quads = jnp.where(c == 0, quads, quads[:, ::-1])
    quads = jnp.where(zh == 0, quads, quads[::-1])
    block = quads.reshape(BLK, HALF)
    x_theirs, block, mine = barrier((x_theirs, block, mine))
    near = [send(block, first_by(-j)) for j in (1, 2, 3)]

    out = partial_blocks(at, mine, x_theirs, g_mine, g_theirs)
    out, near = barrier((out, near))

    line = jnp.stack([block] + near)
    some = jnp.where(zl % 2 == 0, jnp.stack([block, near[0]]), jnp.stack(near[1:]))
    far = [send(some, second_by(-j)) for j in (1, 2, 3)]
    out = list(out)
    out[2], far[1] = barrier((out[2], far[1]))
    got2, got1, got3 = (send(out[j], first_by(j)) for j in (2, 1, 3))
    far_a, far_b = jnp.stack([f[0] for f in far]), jnp.stack([f[1] for f in far])
    parts = [far_a, far_b, send(far_a, z_by(-1)), send(far_b, z_by(1))]

    sums = sum_blocks(at, [out[0], got1, got2, got3])
    column = [sums[0]] + [send(sums[j], second_by(j)) for j in (1, 2, 3)]
    column[1], line, parts = barrier((column[1], line, parts))
    units = unit_sums(column)
    swapped = [send(p, other_core) for p in [line] + parts]
    keys, input_grad = products(at, normed, key_grad, [line] + parts, swapped)
    units = lax.all_to_all(units, ("zh", "zl", "c"), 0, 0, tiled=True)
    units, keys, input_grad = barrier((units, keys, input_grad))
    piece = jnp.sum(units.reshape(8, 2, 72, 128).astype(jnp.float32), axis=0)
    ring = jnp.stack([piece] + [send(piece, zl_by(-j)) for j in (1, 2, 3)])
    ring = lax.dynamic_slice_in_dim(jnp.concatenate([ring, ring]), (4 - zl) % 4, 4, axis=0)
    weight_grad = ring.transpose(2, 1, 0, 3).reshape(72, KD)
    return keys, input_grad, weight_grad


def solution(mesh):
    fine = Mesh(mesh.devices.reshape(SIZES), AXES)
    fsdp = ("y", "x", "zh", "c")
    tokens, rows = P(AXES, None), P(fsdp, None)
    return jax.shard_map(
        local,
        mesh=fine,
        in_specs=(tokens, rows, tokens),
        out_specs=(tokens, tokens, rows),
        check_vma=False,
    )
```

```python
import jax
import jax.numpy as jnp
from jax import lax
from jax.experimental import pallas as pl
from jax.experimental.pallas import tpu as pltpu
from jax.sharding import Mesh, PartitionSpec as P

GROUP = 128
TAIL = 32
AXES = ("zl", "y", "x", "zh", "c")
SIZES = (4, 4, 4, 2, 2)
TOK = 256
D = 4608
KD = 1024
HALF = KD // 2
BLK = D // 16
VMEM_LIMIT = 28 * 1024 * 1024
SMALL_LIMIT = 20 * 1024 * 1024


barrier = lax.optimization_barrier


def in_hbm(x):
    return pltpu.with_memory_space_constraint(x, pltpu.HBM)


def pairs(move):
    out = []
    for i in range(256):
        rest, at = i, {}
        for name, size in zip(reversed(AXES), reversed(SIZES)):
            at[name] = rest % size
            rest //= size
        to = move(dict(at))
        j = 0
        for name, size in zip(AXES, SIZES):
            j = j * size + to[name] % size
        out.append((i, j))
    return out


def send(value, move):
    return lax.ppermute(value, AXES, pairs(move))


def other_core(at):
    at["c"] ^= 1
    return at


def mirror(at):
    at["zh"] ^= 1
    at["zl"] = 3 - at["zl"]
    return at


def first_by(step):
    def move(at):
        at["x" if at["c"] == 0 else "y"] += step
        return at

    return move


def second_by(step):
    def move(at):
        at["y" if at["c"] == 0 else "x"] += step
        return at

    return move


def z_by(step):
    def move(at):
        z = (4 * at["zh"] + at["zl"] + step) % 8
        at["zh"], at["zl"] = z // 4, z % 4
        return at

    return move


def zl_by(step):
    def move(at):
        at["zl"] += step
        return at

    return move


def restored(x):
    v = x.astype(jnp.float32).T
    scale = jnp.max(jnp.abs(v), axis=0, keepdims=True)
    low = (0.25 * scale).astype(jnp.bfloat16).astype(jnp.float32)
    high = (0.75 * scale).astype(jnp.bfloat16).astype(jnp.float32)
    twice = v + v
    mag = jnp.where((twice >= scale) | (twice < -scale), high, low)
    r = jnp.where(v >= 0.0, mag, -mag)
    token = lax.broadcasted_iota(jnp.int32, r.shape, 1)
    return jnp.where(token >= TOK - TAIL, v, r).astype(jnp.bfloat16)


def quantize_kernel(x_ref, out_ref):
    for g in range(x_ref.shape[1] // GROUP):
        span = slice(g * GROUP, (g + 1) * GROUP)
        out_ref[span, :] = restored(x_ref[:, span])


def quantize(normed):
    width = 6 * GROUP
    return pl.pallas_call(
        quantize_kernel,
        grid=(D // width,),
        in_specs=[pl.BlockSpec((TOK, width), lambda i: (0, i))],
        out_specs=pl.BlockSpec((width, TOK), lambda i: (i, 0)),
        out_shape=jax.ShapeDtypeStruct((D, TOK), jnp.bfloat16),
        compiler_params=pltpu.CompilerParams(vmem_limit_bytes=SMALL_LIMIT),
        cost_estimate=pl.CostEstimate(flops=2 * D * HALF * TOK, bytes_accessed=4 * D * TOK, transcendentals=0),
    )(normed)


ROWS = D // 4


def partial_kernel(at_ref, mine_ref, theirs_ref, gmine_ref, gtheirs_ref, o0, o1, o2, o3, acc, r, sem):
    first, core = at_ref[0], at_ref[2]
    outs = (o0, o1, o2, o3)

    def rows(block):
        return acc.at[block * BLK : (block + 1) * BLK, :]

    def make(step):
        span = slice(step * ROWS, (step + 1) * ROWS)
        total = jnp.dot(mine_ref[...], gmine_ref[...], preferred_element_type=jnp.float32)
        quantize_kernel(theirs_ref, r)
        total += jnp.dot(r[...], gtheirs_ref[...], preferred_element_type=jnp.float32)
        acc[span, :] = total.astype(jnp.bfloat16)
        for b in range(4 * step, 4 * step + 4):
            to = jnp.where(core == 0, b % 4, b // 4)
            place = jnp.where(core == 0, b // 4, b % 4)
            ahead = lax.rem(to + 4 - first, 4)
            for j, out in enumerate(outs):

                @pl.when(ahead == j)
                def _():
                    pltpu.make_async_copy(rows(b), out.at[place], sem.at[b]).start()

    for step in range(4):

        @pl.when(pl.program_id(0) == step)
        def _():
            make(step)

    @pl.when(pl.program_id(0) == 3)
    def _():
        for b in range(16):
            pltpu.make_async_copy(rows(b), o0.at[0], sem.at[b]).wait()


def partial_blocks(at, mine, theirs, gmine, gtheirs):
    acts = pl.BlockSpec((ROWS, TOK), lambda i, at: (i, 0))
    grads = pl.BlockSpec((TOK, HALF), lambda i, at: (0, 0))
    return pl.pallas_call(
        partial_kernel,
        grid_spec=pltpu.PrefetchScalarGridSpec(
            num_scalar_prefetch=1,
            grid=(4,),
            in_specs=[acts, pl.BlockSpec((TOK, ROWS), lambda i, at: (0, i)), grads, grads],
            out_specs=[pl.BlockSpec(memory_space=pl.ANY)] * 4,
            scratch_shapes=[
                pltpu.VMEM((D, HALF), jnp.bfloat16),
                pltpu.VMEM((ROWS, TOK), jnp.bfloat16),
                pltpu.SemaphoreType.DMA((16,)),
            ],
        ),
        out_shape=[jax.ShapeDtypeStruct((4, BLK, HALF), jnp.bfloat16)] * 4,
        compiler_params=pltpu.CompilerParams(vmem_limit_bytes=SMALL_LIMIT),
        cost_estimate=pl.CostEstimate(flops=3 * 4 * D * HALF * TOK, bytes_accessed=10 * 2**20, transcendentals=0),
    )(at, mine, theirs, gmine, gtheirs)


def sum_kernel(at_ref, a, b, c, d, r0, r1, r2, r3):
    total = a[0].astype(jnp.float32) + b[0].astype(jnp.float32) + c[0].astype(jnp.float32) + d[0].astype(jnp.float32)
    for j, r in enumerate((r0, r1, r2, r3)):

        @pl.when(pl.program_id(0) == j)
        def _():
            r[...] = total.astype(r.dtype)


def sum_blocks(at, blocks):
    spec = pl.BlockSpec((1, BLK, HALF), lambda j, at: (lax.rem(at[1] + j, 4), 0, 0))
    return pl.pallas_call(
        sum_kernel,
        grid_spec=pltpu.PrefetchScalarGridSpec(
            num_scalar_prefetch=1,
            grid=(4,),
            in_specs=[spec] * 4,
            out_specs=[pl.BlockSpec((BLK, HALF), lambda j, at: (0, 0))] * 4,
        ),
        out_shape=[jax.ShapeDtypeStruct((BLK, HALF), jnp.bfloat16 if j else jnp.float32) for j in range(4)],
        compiler_params=pltpu.CompilerParams(vmem_limit_bytes=SMALL_LIMIT),
        cost_estimate=pl.CostEstimate(flops=0, bytes_accessed=6 * 2**20, transcendentals=0),
    )(at, *blocks)


def units_kernel(a, b, c, d, out_ref, total):
    total[...] = a[...] + b[...].astype(jnp.float32) + c[...].astype(jnp.float32) + d[...].astype(jnp.float32)
    for zh in range(2):
        for core in range(2):
            for zl in range(4):
                s = 72 * (2 * zh + core)
                out_ref[8 * zh + 2 * zl + core] = total[s : s + 72, 128 * zl : 128 * (zl + 1)].astype(jnp.bfloat16)


def unit_sums(column):
    vmem = pl.BlockSpec(memory_space=pltpu.VMEM)
    return pl.pallas_call(
        units_kernel,
        in_specs=[vmem] * 4,
        out_specs=vmem,
        out_shape=jax.ShapeDtypeStruct((16, 72, 128), jnp.bfloat16),
        scratch_shapes=[pltpu.VMEM((BLK, HALF), jnp.float32)],
        compiler_params=pltpu.CompilerParams(vmem_limit_bytes=SMALL_LIMIT),
        cost_estimate=pl.CostEstimate(flops=0, bytes_accessed=2 * 2**20, transcendentals=0),
    )(*column)


def product_kernel(at_ref, x_ref, g_ref, *rest):
    sides, (keys_ref, grad_ref, w, x, g, total, sem, x_sem, g_sem) = (rest[:5], rest[5:10]), rest[10:]
    step, core = pl.program_id(0), at_ref[2]
    x_at, y_at = jnp.where(core == 0, at_ref[0], at_ref[1]), jnp.where(core == 0, at_ref[1], at_ref[0])
    turn = 2 * (at_ref[3] & 1)

    def quarter(i):
        return pl.ds(pl.multiple_of(((y_at + turn + i) & 3) * ROWS, ROWS), ROWS)

    def fetch(i):
        return pltpu.make_async_copy(x_ref.at[:, quarter(i)], x.at[:, quarter(i)], x_sem.at[i])

    def copy(source, dy, dx, side, i):
        block = 4 * ((y_at + dy) & 3) + ((x_at + dx) & 3)
        rows = pl.ds(pl.multiple_of(block * BLK, BLK), BLK)
        columns = slice(side * HALF, (side + 1) * HALF)
        return pltpu.make_async_copy(source, w.at[rows, columns], sem.at[side, i])

    def start(side, line, parts, i):
        ahead = (turn + i) & 3
        if side == 1:
            copy(line.at[ahead], ahead, 0, side, i).start()
            for m in range(1, 4):
                copy(parts[i].at[m - 1], ahead, m, side, i).start()
            return

        @pl.when(ahead == 0)
        def _():
            for m in range(4):
                copy(line.at[m], 0, m, side, i).start()

        @pl.when(ahead != 0)
        def _():
            for m in range(4):
                copy(parts[m].at[jnp.maximum(ahead - 1, 0)], ahead, turn + m, side, i).start()

    @pl.when(step == 0)
    def _():
        pltpu.make_async_copy(g_ref, g, g_sem).start()
        for own in range(2):

            @pl.when(core == own)
            def _():
                for i in range(4):
                    fetch(i).start()
                    for side in range(2):
                        mine = sides[0 if side == own else 1]
                        start(side, mine[0], mine[1:], i)

        total[...] = jnp.zeros_like(total)
        pltpu.make_async_copy(g_ref, g, g_sem).wait()

    fetch(step).wait()
    rows = quarter(step)
    for side in range(2):
        part = w.at[rows, side * HALF : (side + 1) * HALF]
        pltpu.make_async_copy(part, part, sem.at[side, step]).wait()
    part = w[rows, :]
    total[...] += jnp.dot(x[:, rows], part, preferred_element_type=jnp.float32)
    grad = lax.dot_general(g[...], part, (((1,), (1,)), ((), ())), preferred_element_type=jnp.float32)
    grad_ref[...] = grad.astype(grad_ref.dtype)

    @pl.when(step == pl.num_programs(0) - 1)
    def _():
        keys_ref[...] = total[...].astype(jnp.bfloat16)


def products(at, normed, key_grad, parts, swapped):
    def across(i, at):
        y = jnp.where(at[2] == 0, at[1], at[0])
        return (0, lax.rem(y + 2 * lax.rem(at[3], 2) + i, 4))

    whole = lambda i, at: (0, 0)
    return pl.pallas_call(
        product_kernel,
        grid_spec=pltpu.PrefetchScalarGridSpec(
            num_scalar_prefetch=1,
            grid=(4,),
            in_specs=[pl.BlockSpec(memory_space=pl.ANY)] * 12,
            out_specs=[pl.BlockSpec((TOK, KD), whole), pl.BlockSpec((TOK, ROWS), across)],
            scratch_shapes=[
                pltpu.VMEM((D, KD), jnp.bfloat16),
                pltpu.VMEM((TOK, D), jnp.bfloat16),
                pltpu.VMEM((TOK, KD), jnp.bfloat16),
                pltpu.VMEM((TOK, KD), jnp.float32),
                pltpu.SemaphoreType.DMA((2, 4)),
                pltpu.SemaphoreType.DMA((4,)),
                pltpu.SemaphoreType.DMA,
            ],
        ),
        out_shape=[jax.ShapeDtypeStruct((TOK, KD), jnp.bfloat16), jax.ShapeDtypeStruct((TOK, D), jnp.bfloat16)],
        compiler_params=pltpu.CompilerParams(vmem_limit_bytes=VMEM_LIMIT),
        cost_estimate=pl.CostEstimate(flops=4 * D * KD * TOK, bytes_accessed=14 * 2**20, transcendentals=0),
    )(at, in_hbm(normed), in_hbm(key_grad), *parts, *swapped)


def local(normed, key_weight, key_grad):
    zl, y, x, zh, c = (lax.axis_index(name) for name in AXES)
    first, second = jnp.where(c == 0, x, y), jnp.where(c == 0, y, x)
    at = jnp.stack([first, second, c, zl]).astype(jnp.int32)

    def half(a, which):
        return lax.dynamic_slice_in_dim(a, which * HALF, HALF, axis=1)

    w_mine, w_theirs = half(key_weight, c), half(key_weight, 1 - c)
    g_mine, g_other = half(key_grad, c), half(key_grad, 1 - c)
    x_theirs = send(normed, other_core)
    g_theirs = send(g_other, other_core)
    w_core = send(w_theirs, other_core)
    w_mirror = send(w_mine, mirror)
    w_both = send(w_theirs, lambda at: other_core(mirror(at)))
    mine = quantize(normed)
    w_core, w_mirror, w_both, mine = barrier((w_core, w_mirror, w_both, mine))
    quads = jnp.stack([w_mine, w_core, w_mirror, w_both]).reshape(2, 2, 72, HALF)
    quads = jnp.where(c == 0, quads, quads[:, ::-1])
    quads = jnp.where(zh == 0, quads, quads[::-1])
    block = quads.reshape(BLK, HALF)
    x_theirs, block, mine = barrier((x_theirs, block, mine))
    near = [send(block, first_by(-j)) for j in (1, 2, 3)]

    out = partial_blocks(at, mine, x_theirs, g_mine, g_theirs)
    out, near = barrier((out, near))

    line = jnp.stack([block] + near)
    some = jnp.where(zl % 2 == 0, jnp.stack([block, near[0]]), jnp.stack(near[1:]))
    far = [send(some, second_by(-j)) for j in (1, 2, 3)]
    out = list(out)
    out[2], far[1] = barrier((out[2], far[1]))
    got2, got1, got3 = (send(out[j], first_by(j)) for j in (2, 1, 3))
    far_a, far_b = jnp.stack([f[0] for f in far]), jnp.stack([f[1] for f in far])
    parts = [far_a, far_b, send(far_a, z_by(-1)), send(far_b, z_by(1))]

    sums = sum_blocks(at, [out[0], got1, got2, got3])
    far_sum = send(sums[2], second_by(2))
    far_sum, line, parts = barrier((far_sum, line, parts))
    column = [sums[0], far_sum, send(sums[1], second_by(1)), send(sums[3], second_by(3))]
    units = unit_sums(column)
    swapped = [send(p, other_core) for p in [line] + parts]
    keys, input_grad = products(at, normed, key_grad, [line] + parts, swapped)
    units = lax.all_to_all(units, ("zh", "zl", "c"), 0, 0, tiled=True)
    units, keys, input_grad = barrier((units, keys, input_grad))
    piece = jnp.sum(units.reshape(8, 2, 72, 128).astype(jnp.float32), axis=0)
    ring = jnp.stack([piece] + [send(piece, zl_by(-j)) for j in (1, 2, 3)])
    ring = lax.dynamic_slice_in_dim(jnp.concatenate([ring, ring]), (4 - zl) % 4, 4, axis=0)
    weight_grad = ring.transpose(2, 1, 0, 3).reshape(72, KD)
    return keys, input_grad, weight_grad


def solution(mesh):
    fine = Mesh(mesh.devices.reshape(SIZES), AXES)
    fsdp = ("y", "x", "zh", "c")
    tokens, rows = P(AXES, None), P(fsdp, None)
    return jax.shard_map(
        local,
        mesh=fine,
        in_specs=(tokens, rows, tokens),
        out_specs=(tokens, tokens, rows),
        check_vma=False,
    )
```
